256 devices in a mesh: grp: 2 (over x_hi), seq: 128 (over y, z, x_lo, core).
Axes of the slice: x: 4 (x_hi: 2, x_lo: 2; x = x_hi * 2 + x_lo), y: 4, z: 8, core: 2. Of those that a mesh axis runs over, the one named last changes fastest.
Arguments:
- teach_q: bfloat16 [2, 16384, 1536], P('grp', 'seq'), may hold values from -60 to 60
- teach_k: bfloat16 [2, 16384, 1536], P('grp', 'seq'), may hold values from -6 to 6
- teach_v: bfloat16 [2, 16384, 1536], P('grp', 'seq'), may hold values from -6 to 6
- teach_resid: bfloat16 [2, 16384, 1536], P('grp', 'seq'), may hold values from -1400 to 1400
- teach_out_w: bfloat16 [1536, 1536], P('grp'), may hold values from -0.15625 to 0.15625
- teach_head_w: bfloat16 [1536, 1024], P('grp'), may hold values from -0.4375 to 0.4375
- teach_head_bias: float32 [1024], replicated, may hold values from -6 to 6
- stud_q: bfloat16 [2, 16384, 1024], P('grp', 'seq'), may hold values from -60 to 60
- stud_k: bfloat16 [2, 16384, 1024], P('grp', 'seq'), may hold values from -6 to 6
- stud_v: bfloat16 [2, 16384, 1024], P('grp', 'seq'), may hold values from -6 to 6
- stud_resid: bfloat16 [2, 16384, 1024], P('grp', 'seq'), may hold values from -1400 to 1400
- stud_out_w: bfloat16 [1024, 1024], P('grp'), may hold values from -0.1875 to 0.1875
- stud_head_w: bfloat16 [1024, 1024], P('grp'), may hold values from -0.5 to 0.5
- stud_head_bias: float32 [1024], replicated, may hold values from -6 to 6
- lengths: int32 [2], replicated, may hold values from 8192 to 16384, as said below
- align: int32 [2, 16384], P('grp', 'seq'), may hold values from 0 to 16383, as said below
Outputs:
- grad_q: bfloat16 [2, 16384, 1024], P('grp', 'seq')
- grad_k: bfloat16 [2, 16384, 1024], P('grp', 'seq')
- grad_v: bfloat16 [2, 16384, 1024], P('grp', 'seq')
The draws below stay inside these ranges and needn't reach their ends.
Inputs may be any that keep to these rules, and one draw needn't show every extreme that they name: `lengths`: one of the two utterances has all 16384 frames; the other is shorter. t - 16 <= align[g, t] <= t; in each row some frame has align[g, t] = t - 16.
All inputs are finite; a program needn't handle non-finite values.
Results may differ from the reference program's by a relative error of at most 0.023.
Values may be sent and summed in bfloat16 or wider, within the bound.
A program may use at most 128 MiB of HBM per device.

```python
import math
import jax
import jax.numpy as jnp
from jax import lax

DT = 1536
HT = 24
DS = 1024
HS = 16
HD = 64
VOCAB = 1024
CTX = 512
MAXD = 16
FRAMES = 16384


def attention_pattern(key, width):
    key_base = jax.random.fold_in(key, 0)
    keys_base = jax.random.truncated_normal(key_base, -6.0, 6.0, (2, FRAMES, width), jnp.float32)
    return keys_base


def drawn_queries(key, width, salt):
    key = jax.random.fold_in(key, salt)
    drawn = jax.random.truncated_normal(key, -6.0, 6.0, (2, FRAMES, width), jnp.float32)
    return drawn.astype(jnp.bfloat16)


def drawn_keys(key, width):
    keys_base = attention_pattern(key, width)
    keys_out = keys_base
    return keys_out.astype(jnp.bfloat16)


def residual_rows(key, width):
    key_main = jax.random.fold_in(key, 0)
    drawn = jax.random.truncated_normal(key_main, -6.0, 6.0, (2, FRAMES, width), jnp.float32)
    return drawn.astype(jnp.bfloat16)


def draw_teach_q(key, part):
    return drawn_queries(jax.random.fold_in(key, 100), DT, 1)


def draw_teach_k(key, part):
    return drawn_keys(jax.random.fold_in(key, 100), DT)


def draw_stud_q(key, part):
    return drawn_queries(jax.random.fold_in(key, 200), DS, 2)


def draw_stud_k(key, part):
    return drawn_keys(jax.random.fold_in(key, 200), DS)


def draw_teach_resid(key, part):
    key = jax.random.fold_in(key, 3)
    return residual_rows(key, DT)


def draw_stud_resid(key, part):
    key = jax.random.fold_in(key, 4)
    return residual_rows(key, DS)


def draw_lengths(key, part):
    key = jax.random.fold_in(key, 7)
    key_short, key_which = jax.random.split(key)
    shorter = jax.random.randint(key_short, (), FRAMES // 2, FRAMES, jnp.int32)
    which = jax.random.randint(key_which, (), 0, 2, jnp.int32)
    return jnp.where(jnp.arange(2, dtype=jnp.int32) == which, FRAMES, shorter).astype(jnp.int32)


def draw_align(key, part):
    key = jax.random.fold_in(key, 9)
    key_delay, key_where = jax.random.split(key)
    delays = jax.random.randint(key_delay, (2, FRAMES), 0, MAXD + 1, jnp.int32)
    forced = jax.random.randint(key_where, (2, 1), MAXD, FRAMES - 1, jnp.int32)
    frame_index = jnp.arange(FRAMES, dtype=jnp.int32)[None, :]
    delays = jnp.where(frame_index == forced, MAXD, delays)
    delays = jnp.where(frame_index == FRAMES - 1, 0, delays)
    return jnp.maximum(frame_index - delays, 0).astype(jnp.int32)


def levels(own_key, extent, shards, smallest, largest):
    gain, own = 1.0, jax.random.fold_in(own_key, 6)
    for dim, parts in shards:
        steps = jnp.exp(jax.random.uniform(jax.random.fold_in(own, dim), (parts,), jnp.float32, smallest / len(shards), largest / len(shards)))
        gain = gain * jnp.repeat(steps, extent[dim] // parts).reshape([-1 if axis == dim else 1 for axis in range(len(extent))])
    return gain


def noise(rng, shape, scale, most, shards=(), held_as=jnp.bfloat16):
    result = jax.random.normal(rng, shape, jnp.float32) * scale
    if len(shards) > 0:
        result = levels(rng, shape, shards, -0.22, 0.18) * result
    return jnp.clip(result, min=-most, max=most).astype(held_as)


def setup_inputs(seed: int = 0) -> dict:
    splits = jax.random.split(jax.random.key(seed), 17)
    return {
        "teach_q": draw_teach_q(jax.random.fold_in(splits[16], 71), 0),
        "teach_k": draw_teach_k(jax.random.fold_in(splits[16], 71), 0),
        "teach_v": noise(splits[2], (2, FRAMES, DT), 1.0, 6.0, ((0, 2), (1, 128))),
        "teach_resid": draw_teach_resid(jax.random.fold_in(splits[16], 71), 0),
        "teach_out_w": noise(splits[4], (DT, DT), DT ** -0.5, 0.15625, ((0, 2),)),
        "teach_head_w": noise(splits[5], (DT, VOCAB), (DT // 9) ** -0.5, 0.4375, ((0, 2),)),
        "teach_head_bias": noise(splits[6], (VOCAB,), 1.0, 6.0, (), jnp.float32),
        "stud_q": draw_stud_q(jax.random.fold_in(splits[16], 71), 0),
        "stud_k": draw_stud_k(jax.random.fold_in(splits[16], 71), 0),
        "stud_v": noise(splits[9], (2, FRAMES, DS), 1.0, 6.0, ((0, 2), (1, 128))),
        "stud_resid": draw_stud_resid(jax.random.fold_in(splits[16], 71), 0),
        "stud_out_w": noise(splits[11], (DS, DS), DS ** -0.5, 0.1875, ((0, 2),)),
        "stud_head_w": noise(splits[12], (DS, VOCAB), (DS // 9) ** -0.5, 0.5, ((0, 2),)),
        "stud_head_bias": noise(splits[13], (VOCAB,), 1.0, 6.0, (), jnp.float32),
        "lengths": draw_lengths(jax.random.fold_in(splits[16], 71), 0),
        "align": draw_align(jax.random.fold_in(splits[16], 71), 0),
    }


score_scale = 0.125
grad_scale = 16.0
mask_fill = -1e30


def window_probs(query_rows, key_rows, head_count, query_pos, key_pos, length):
    row_count = query_rows.shape[0]
    key_count = key_rows.shape[0]
    query_heads = query_rows.astype(jnp.float32).reshape(row_count, head_count, HD)
    key_heads = key_rows.astype(jnp.float32).reshape(key_count, head_count, HD)
    scores = jnp.einsum("thd,shd->hts", query_heads, key_heads) * score_scale
    allowed = (key_pos[None, :] <= query_pos[:, None]) & (key_pos[None, :] >= query_pos[:, None] - CTX)
    allowed = allowed & (key_pos[None, :] >= 0) & (key_pos[None, :] < length)
    scores = jnp.where(allowed[None], scores, mask_fill)
    row_max = jnp.max(scores, axis=-1, keepdims=True)
    exp_scores = jnp.exp(scores - row_max)
    return exp_scores / jnp.sum(exp_scores, axis=-1, keepdims=True)


def mix_values(probs, value_rows, head_count):
    rounded = lax.optimization_barrier(probs.astype(jnp.bfloat16)).astype(jnp.float32)
    value_heads = value_rows.astype(jnp.float32).reshape(value_rows.shape[0], head_count, HD)
    context = jnp.einsum("hts,shd->thd", rounded, value_heads)
    return context.reshape(context.shape[0], head_count * HD).astype(jnp.bfloat16), rounded


def padded(rows):
    return jnp.concatenate([jnp.zeros((CTX, rows.shape[1]), rows.dtype), rows], axis=0)


def teacher_posteriors(query, keys, values, resid, out_w, head_w, bias, length):
    block_rows = math.gcd(FRAMES, 512)
    block_count = FRAMES // block_rows
    keys_padded = padded(keys)
    values_padded = padded(values)

    def one_block(block_index):
        first = block_index * block_rows
        query_rows = lax.dynamic_slice_in_dim(query, first, block_rows, 0)
        key_rows = lax.dynamic_slice_in_dim(keys_padded, first, block_rows + CTX, 0)
        value_rows = lax.dynamic_slice_in_dim(values_padded, first, block_rows + CTX, 0)
        resid_rows = lax.dynamic_slice_in_dim(resid, first, block_rows, 0)
        query_pos = first + jnp.arange(block_rows, dtype=jnp.int32)
        key_pos = first - CTX + jnp.arange(block_rows + CTX, dtype=jnp.int32)
        probs = window_probs(query_rows, key_rows, HT, query_pos, key_pos, length)
        context, rounded = mix_values(probs, value_rows, HT)
        hidden = (resid_rows.astype(jnp.float32) + jnp.dot(context, out_w, preferred_element_type=jnp.float32)).astype(jnp.bfloat16)
        logits = jnp.dot(hidden, head_w, preferred_element_type=jnp.float32) + bias
        return jax.nn.softmax(logits, axis=-1).astype(jnp.bfloat16)

    blocks = lax.map(one_block, jnp.arange(block_count, dtype=jnp.int32))
    return blocks.reshape(FRAMES, VOCAB)


def student_grads(query, keys, values, resid, out_w, head_w, bias, length, targets):
    block_rows = math.gcd(FRAMES, 512)
    block_count = FRAMES // block_rows
    keys_padded = padded(keys)
    values_padded = padded(values)

    def one_block(carry, block_index):
        key_buffer, value_buffer = carry
        first = block_index * block_rows
        query_rows = lax.dynamic_slice_in_dim(query, first, block_rows, 0)
        key_rows = lax.dynamic_slice_in_dim(keys_padded, first, block_rows + CTX, 0)
        value_rows = lax.dynamic_slice_in_dim(values_padded, first, block_rows + CTX, 0)
        resid_rows = lax.dynamic_slice_in_dim(resid, first, block_rows, 0)
        target_rows = lax.dynamic_slice_in_dim(targets, first, block_rows, 0).astype(jnp.float32)
        query_pos = first + jnp.arange(block_rows, dtype=jnp.int32)
        key_pos = first - CTX + jnp.arange(block_rows + CTX, dtype=jnp.int32)
        probs = window_probs(query_rows, key_rows, HS, query_pos, key_pos, length)
        context, rounded = mix_values(probs, value_rows, HS)
        hidden = (resid_rows.astype(jnp.float32) + jnp.dot(context, out_w, preferred_element_type=jnp.float32)).astype(jnp.bfloat16)
        logits = jnp.dot(hidden, head_w, preferred_element_type=jnp.float32) + bias
        predicted = jax.nn.softmax(logits, axis=-1)
        valid_rows = (query_pos < length).astype(jnp.float32)
        target_sum = jnp.sum(target_rows, axis=-1, keepdims=True)
        logit_grad = (grad_scale * valid_rows[:, None] * (target_sum * predicted - target_rows)).astype(jnp.bfloat16)
        hidden_grad = jnp.dot(logit_grad, head_w.T, preferred_element_type=jnp.float32).astype(jnp.bfloat16)
        mix_grad = jnp.dot(hidden_grad, out_w.T, preferred_element_type=jnp.float32).astype(jnp.bfloat16)
        mix_heads = mix_grad.astype(jnp.float32).reshape(block_rows, HS, HD)
        value_heads = value_rows.astype(jnp.float32).reshape(block_rows + CTX, HS, HD)
        key_heads = key_rows.astype(jnp.float32).reshape(block_rows + CTX, HS, HD)
        query_heads = query_rows.astype(jnp.float32).reshape(block_rows, HS, HD)
        prob_grad = jnp.einsum("thd,shd->hts", mix_heads, value_heads)
        value_grad = jnp.einsum("hts,thd->shd", rounded, mix_heads).reshape(block_rows + CTX, DS)
        inner_sum = jnp.sum(probs * prob_grad, axis=-1, keepdims=True)
        score_grad = (score_scale * probs * (prob_grad - inner_sum)).astype(jnp.bfloat16)
        score_grad = lax.optimization_barrier(score_grad).astype(jnp.float32)
        query_grad = jnp.einsum("hts,shd->thd", score_grad, key_heads).reshape(block_rows, DS).astype(jnp.bfloat16)
        key_grad = jnp.einsum("hts,thd->shd", score_grad, query_heads).reshape(block_rows + CTX, DS)
        old_keys = lax.dynamic_slice_in_dim(key_buffer, first, block_rows + CTX, 0)
        old_values = lax.dynamic_slice_in_dim(value_buffer, first, block_rows + CTX, 0)
        key_buffer = lax.dynamic_update_slice_in_dim(key_buffer, old_keys + key_grad, first, 0)
        value_buffer = lax.dynamic_update_slice_in_dim(value_buffer, old_values + value_grad, first, 0)
        return (key_buffer, value_buffer), query_grad

    empty = jnp.zeros((FRAMES + CTX, DS), jnp.float32)
    (key_buffer, value_buffer), query_blocks = lax.scan(one_block, (empty, empty), jnp.arange(block_count, dtype=jnp.int32))
    return (query_blocks.reshape(FRAMES, DS), key_buffer[CTX:].astype(jnp.bfloat16), value_buffer[CTX:].astype(jnp.bfloat16))


def reference(teach_q, teach_k, teach_v, teach_resid, teach_out_w, teach_head_w, teach_head_bias, stud_q, stud_k, stud_v, stud_resid, stud_out_w, stud_head_w, stud_head_bias, lengths, align):
    posterior = [teacher_posteriors(teach_q[source], teach_k[source], teach_v[source], teach_resid[source], teach_out_w, teach_head_w, teach_head_bias, lengths[source]) for source in range(2)]
    query_out = []
    key_out = []
    value_out = []
    for holder in range(2):
        source = 1 - holder
        targets = jnp.take(posterior[source], align[holder], axis=0)
        query_grad, key_grad, value_grad = student_grads(stud_q[holder], stud_k[holder], stud_v[holder], stud_resid[holder], stud_out_w, stud_head_w, stud_head_bias, lengths[source], targets)
        query_out.append(query_grad)
        key_out.append(key_grad)
        value_out.append(value_grad)
    return (jnp.stack(query_out), jnp.stack(key_out), jnp.stack(value_out))
```

```python
import functools

import jax
import jax.numpy as jnp
from jax import lax
from jax.experimental import pallas as pl
from jax.experimental.pallas import tpu as pltpu
from jax.sharding import PartitionSpec as P

CTX = 512
MAXD = 16
R = 128
WIN = CTX + R
DT = 1536
DS = 1024
VOCAB = 1024
TP = DT // 128
SP = DS // 128
CW = 256
PPC = CW // 128
TCH = DT // CW
SCH = DS // CW
NCH = TCH + SCH
NY = 4

FILL = -1e30
F32 = jnp.float32
BF16 = jnp.bfloat16
MESH = pl.DeviceIdType.MESH
NT = (((1,), (1,)), ((), ()))
NN = (((1,), (0,)), ((), ()))


def mm(a, b, dims=NN):
    return lax.dot_general(a, b, dims, preferred_element_type=F32)


def cols(i, width):
    return pl.ds(pl.multiple_of(i * width, width), width)


class Cast:
    def __init__(self, place, send, recv, group, seq, zdev, xdev, cdev, xl, core):
        self.place, self.send, self.recv = place, send, recv
        self.g, self.zdev, self.xdev, self.cdev = group, zdev, xdev, cdev
        self.xl, self.core = xl, core

    def copy(self, kind, chunk):
        if kind == 0:
            src, dst, dev = 0, 4, self.zdev
        elif kind == 1:
            src, dst, dev = 4 * self.xl, 2, self.xdev
        elif kind == 2:
            src, dst, dev = 4 * self.core, 1 + 2 * self.core, self.cdev
        else:
            src, dst, dev = 2, 3 - 2 * self.core, self.cdev
        return pltpu.make_async_remote_copy(
            src_ref=self.place(src, chunk),
            dst_ref=self.place(dst, chunk),
            send_sem=self.send.at[kind, chunk],
            recv_sem=self.recv.at[kind, chunk],
            device_id=(self.g, dev),
            device_id_type=MESH,
        )

    def start(self, chunk):
        self.copy(0, chunk).start()

    def landed(self, kind, chunk):
        dist = (4, 2, 3 - 2 * self.core, 1 + 2 * self.core)[kind]
        ref = self.place(dist, chunk)
        pltpu.make_async_remote_copy(
            src_ref=ref,
            dst_ref=ref,
            send_sem=self.send.at[kind, chunk],
            recv_sem=self.recv.at[kind, chunk],
            device_id=(self.g, self.cdev),
            device_id_type=MESH,
        ).wait_recv()

    def a(self, chunk):
        self.landed(0, chunk)
        self.copy(1, chunk).start()
        self.copy(2, chunk).start()

    def b(self, chunk):
        self.landed(1, chunk)
        self.copy(3, chunk).start()

    def c(self, chunk):
        self.landed(2, chunk)
        self.landed(3, chunk)

    def sent(self, chunk):
        for kind in range(4):
            self.copy(kind, chunk).wait_send()


def kernel(
    ns,
    tq,
    tk,
    tv,
    tr,
    tow,
    thw,
    thb,
    sq,
    sk,
    sv,
    sr,
    sow,
    shw,
    shb,
    lens,
    align,
    gq,
    gk,
    gv,
    kv,
    qt,
    rt,
    rs,
    wt,
    ws,
    qm,
    probs,
    ctx_t,
    ctx_s,
    mix_s,
    hid,
    logits,
    post,
    ext,
    tail,
    lgrad,
    bias_t,
    bias_s,
    bias_k,
    stat_c,
    stat,
    lsem,
    kv_send,
    kv_recv,
    q_send,
    q_recv,
    m_send,
    m_recv,
    s_send,
    s_recv,
    wx_send,
    wx_recv,
    wy_send,
    wy_recv,
    wc_send,
    wc_recv,
    p_send,
    p_recv,
):
    g = lax.axis_index("grp")
    s = lax.axis_index("seq")
    og = 1 - g
    core = lax.rem(s, 2)
    xl = lax.rem(s // 2, 2)
    ystep = ns // NY
    y = s // ystep
    xdev = s + 2 - 4 * xl
    cdev = s + 1 - 2 * core
    ahead = lax.rem(s + 4, ns)
    behind = lax.rem(s + ns - 4, ns)
    ynext = lax.rem(s + ystep, ns)
    yprev = lax.rem(s + ns - ystep, ns)
    s_next = lax.rem(s + 1, ns)
    s_prev = lax.rem(s + ns - 1, ns)

    own = [
        (tk.at[0], kv.at[0, pl.ds(CTX, R), pl.ds(0, DT)]),
        (tv.at[0], kv.at[1, pl.ds(CTX, R), pl.ds(0, DT)]),
        (sk.at[0], kv.at[0, pl.ds(CTX, R), pl.ds(DT, DS)]),
        (sv.at[0], kv.at[1, pl.ds(CTX, R), pl.ds(DT, DS)]),
        (sq.at[0], qm.at[0, pl.ds(0, R), :]),
        (tq.at[0], qt),
        (tr.at[0], rt),
        (sr.at[0], rs),
        (tow, wt.at[pl.ds(pl.multiple_of(g * (DT // 2), DT // 2), DT // 2), pl.ds(0, DT)]),
        (thw, wt.at[pl.ds(pl.multiple_of(g * (DT // 2), DT // 2), DT // 2), pl.ds(DT, VOCAB)]),
        (sow, ws.at[pl.ds(pl.multiple_of(g * (DS // 2), DS // 2), DS // 2), pl.ds(0, DS)]),
        (shw, ws.at[pl.ds(pl.multiple_of(g * (DS // 2), DS // 2), DS // 2), pl.ds(DS, VOCAB)]),
    ]
    local = [pltpu.make_async_copy(a, b, lsem.at[i]) for i, (a, b) in enumerate(own)]
    for item in local:
        item.start()
    tail[pl.ds(MAXD, R - MAXD), :] = jnp.zeros((R - MAXD, VOCAB), BF16)

    barrier = pltpu.get_barrier_semaphore()
    peers = [
        (g, xdev),
        (g, cdev),
        (g, ahead),
        (g, behind),
        (g, ynext),
        (g, yprev),
        (og, xdev),
        (og, s),
        (og, s_next),
        (og, s_prev),
    ]
    for peer in peers:
        pl.semaphore_signal(barrier, inc=1, device_id=peer, device_id_type=MESH)
    pl.semaphore_wait(barrier, len(peers))

    def kv_place(dist, chunk):
        return kv.at[:, cols(4 - dist, R), cols(chunk, CW)]

    def q_place(dist, chunk):
        return qm.at[0, cols(dist, R), :]

    def m_place(dist, chunk):
        return qm.at[1, cols(dist, R), cols(chunk, CW)]

    def s_place(dist, chunk):
        return stat.at[:, cols(dist, R)]

    kvc = Cast(kv_place, kv_send, kv_recv, g, s, ahead, xdev, cdev, xl, core)
    back = (g, s, behind, xdev, cdev, 1 - xl, 1 - core)
    qc = Cast(q_place, q_send, q_recv, *back)
    mc = Cast(m_place, m_send, m_recv, *back)
    sc = Cast(s_place, s_send, s_recv, *back)

    def piece(group, owner_y, of, lo=0, n=None):
        depth = (DT if of < 2 else DS) // 16
        half = (DT if of < 2 else DS) // 2
        n = depth if n is None else n
        first = group * half + (owner_y * 2 + core) * depth + lo
        rows = pl.ds(pl.multiple_of(first, 16), n)
        if of == 0:
            return wt.at[rows, pl.ds(0, DT)]
        if of == 1:
            return wt.at[rows, pl.ds(DT, VOCAB)]
        return ws.at[rows, :]

    def across(i):
        source = (tow, thw, sow, shw)[i]
        depth = (DT if i < 2 else DS) // 16
        half = (DT if i < 2 else DS) // 2
        rows = pl.ds(pl.multiple_of((y * 2 + core) * depth, 16), depth)
        there = pl.ds(pl.multiple_of(g * half + (y * 2 + core) * depth, 16), depth)
        dest = (
            wt.at[there, pl.ds(0, DT)],
            wt.at[there, pl.ds(DT, VOCAB)],
            ws.at[there, pl.ds(0, DS)],
            ws.at[there, pl.ds(DS, VOCAB)],
        )[i]
        return pltpu.make_async_remote_copy(
            src_ref=source.at[rows, :],
            dst_ref=dest,
            send_sem=wx_send.at[i],
            recv_sem=wx_recv.at[i],
            device_id=(og, xdev),
            device_id_type=MESH,
        )

    def along(kind, of):
        depth = (DT if of < 2 else DS) // 16
        if kind < 2:
            ref = piece(og, y, of)
        elif kind == 2:
            ref = piece(og, lax.rem(y + NY - 1, NY), of, 0, depth // 2)
        else:
            ref = piece(og, lax.rem(y + 1, NY), of, depth // 2, depth // 2)
        return pltpu.make_async_remote_copy(
            src_ref=ref,
            dst_ref=ref,
            send_sem=wy_send.at[kind, of],
            recv_sem=wy_recv.at[kind, of],
            device_id=(g, (ynext, yprev)[kind % 2]),
            device_id_type=MESH,
        )

    def other_core(step, of):
        ref = piece(og, lax.rem(y + step, NY), of)
        return pltpu.make_async_remote_copy(
            src_ref=ref,
            dst_ref=ref,
            send_sem=wc_send.at[step, of],
            recv_sem=wc_recv.at[step, of],
            device_id=(g, cdev),
            device_id_type=MESH,
        )

    def w_first(of):
        if of < 2:
            across(of).wait_recv()
        else:
            across(2).wait_recv()
            across(3).wait_recv()
        along(0, of).start()
        along(1, of).start()
        other_core(0, of).start()

    def w_second(of):
        along(0, of).wait_recv()
        along(1, of).wait_recv()
        along(2, of).start()
        along(3, of).start()
        other_core(1, of).start()
        other_core(3, of).start()

    def w_third(of):
        along(2, of).wait_recv()
        along(3, of).wait_recv()
        other_core(2, of).start()

    def w_ready(of):
        for step in range(NY):
            other_core(step, of).wait_recv()

    for i in range(4):
        across(i).start()
    local[0].wait()
    local[1].wait()
    for c in range(TCH):
        kvc.start(c)
    local[2].wait()
    local[3].wait()
    for c in range(TCH, NCH):
        kvc.start(c)
    local[4].wait()
    qc.start(0)
    for item in local[5:]:
        item.wait()

    row = lax.broadcasted_iota(jnp.int32, (R, WIN), 0)
    col = lax.broadcasted_iota(jnp.int32, (R, WIN), 1)
    band = (col >= row) & (col <= row + CTX)
    first = s * R
    t_len = lens[g]
    s_len = lens[og]
    key_pos = first - CTX + col
    seen = band & (key_pos >= 0)
    bias_t[...] = jnp.where(seen & (key_pos < t_len), 0.0, FILL)
    bias_s[...] = jnp.where(seen & (key_pos < s_len), 0.0, FILL)
    bias_k[...] = jnp.where(band & (first + col < ns * R) & (first + row < s_len), 0.0, FILL)
    stat_c[...] = jnp.zeros_like(stat_c)

    lane = lax.broadcasted_iota(jnp.int32, (R, 128), 1)
    low = lane < 64

    def stacked(x):
        zero = jnp.zeros_like(x)
        return jnp.concatenate([jnp.where(low, x, zero), jnp.where(low, zero, x)], axis=0)

    def merged(x):
        return jnp.where(low, x[:R], x[R:])

    def scores(q, k, bias):
        sc2 = mm(stacked(q * 0.125), k, NT)
        return sc2.reshape(2, R, WIN) + bias[None]

    def teacher_pair(p):
        at = cols(p, 128)
        x = scores(qt[:, at], kv[0, :, at], bias_t[...])
        top = jnp.max(x, axis=-1, keepdims=True)
        e = jnp.exp(x - top)
        inv = 1.0 / jnp.sum(e, axis=-1, keepdims=True)
        o = mm(e.astype(BF16).reshape(2 * R, WIN), kv[1, :, at])
        o = o * inv.reshape(2 * R, 1)
        ctx_t[:, at] = merged(o).astype(BF16)

    kvc.a(0)

    def teacher_chunk(c, carry):
        kvc.a(c + 1)
        kvc.b(c)

        @pl.when(c == 1)
        def _():
            w_first(0)

        @pl.when(c == 2)
        def _():
            w_first(1)

        @pl.when(c == 3)
        def _():
            w_second(0)

        @pl.when(c == 4)
        def _():
            w_first(2)
            w_third(0)

        @pl.when(c == 5)
        def _():
            w_second(1)

        kvc.c(c)
        for i in range(PPC):
            teacher_pair(c * PPC + i)
        return carry

    lax.fori_loop(0, TCH, teacher_chunk, 0)

    def project(n, tiles, fn):
        def body(i, carry):
            fn(i)
            return carry

        lax.fori_loop(0, tiles, body, 0)

    w_ready(0)

    def t_hidden(i):
        at = cols(i, 256)
        hid[:, at] = (rt[:, at].astype(F32) + mm(ctx_t[...], wt[:, at])).astype(BF16)

    project(0, DT // 256, t_hidden)
    kvc.a(TCH + 1)
    kvc.b(TCH)
    w_third(1)
    w_ready(1)

    def t_logits(i):
        at = cols(i, 256)
        logits[:, at] = mm(hid[...], wt[:, pl.ds(pl.multiple_of(DT + i * 256, 256), 256)]) + thb[:, at]

    project(0, VOCAB // 256, t_logits)
    x = logits[...]
    e = jnp.exp(x - jnp.max(x, axis=-1, keepdims=True))
    post[...] = (e * (1.0 / jnp.sum(e, axis=-1, keepdims=True))).astype(BF16)
    to_body = pltpu.make_async_remote_copy(
        src_ref=post,
        dst_ref=ext,
        send_sem=p_send.at[0],
        recv_sem=p_recv.at[0],
        device_id=(og, s),
        device_id_type=MESH,
    )
    to_tail = pltpu.make_async_remote_copy(
        src_ref=post.at[pl.ds(R - MAXD, MAXD), :],
        dst_ref=tail.at[pl.ds(0, MAXD), :],
        send_sem=p_send.at[1],
        recv_sem=p_recv.at[1],
        device_id=(og, s_next),
        device_id_type=MESH,
    )
    to_body.start()
    to_tail.start()

    def student_pair(j):
        at = cols(TP + j, 128)
        x = scores(qm[0, pl.ds(0, R), cols(j, 128)], kv[0, :, at], bias_s[...])
        top = jnp.max(x, axis=-1, keepdims=True)
        e = jnp.exp(x - top)
        total = jnp.sum(e, axis=-1, keepdims=True)
        pr = e * (1.0 / total)
        probs[j] = pr
        o = mm(pr.astype(BF16).reshape(2 * R, WIN), kv[1, :, at])
        o = merged(o)
        mix_s[:, cols(j, 128)] = o
        ctx_s[:, cols(j, 128)] = o.astype(BF16)
        lse = top + jnp.log(total)
        st = stat_c[...]
        st = jnp.where(lane == 2 * j, lse[0], st)
        stat_c[...] = jnp.where(lane == 2 * j + 1, lse[1], st)

    def student_chunk(c, carry):
        @pl.when(c < NCH - 1)
        def _():
            kvc.a(c + 1)

        kvc.b(c)

        @pl.when(c == TCH + 1)
        def _():
            w_second(2)
            qc.a(0)

        @pl.when(c == TCH + 2)
        def _():
            qc.b(0)

        @pl.when(c == TCH + 3)
        def _():
            w_third(2)

        kvc.c(c)
        for i in range(PPC):
            student_pair((c - TCH) * PPC + i)
        return carry

    kvc.c(TCH)
    for i in range(PPC):
        student_pair(i)
    lax.fori_loop(TCH + 1, NCH, student_chunk, 0)

    w_ready(2)

    def s_hidden(i):
        at = cols(i, 256)
        hid[:, at] = (rs[:, at].astype(F32) + mm(ctx_s[...], ws[:, at])).astype(BF16)

    project(0, DS // 256, s_hidden)

    def s_logits(i):
        at = cols(i, 256)
        w = ws[:, pl.ds(pl.multiple_of(DS + i * 256, 256), 256)]
        logits[:, at] = mm(hid[:, pl.ds(0, DS)], w) + shb[:, at]

    project(0, VOCAB // 256, s_logits)

    rows = jnp.broadcast_to(align[...], (R, R)).T - first
    pick_body = jnp.where(rows == lane, 1.0, 0.0).astype(BF16)
    pick_tail = jnp.where(rows + MAXD == lane, 1.0, 0.0)
    pick_tail = jnp.where(lane < MAXD, pick_tail, 0.0).astype(BF16)
    to_body.wait_recv()
    to_tail.wait_recv()
    targets = mm(pick_body, ext[...]) + mm(pick_tail, tail[...])
    x = logits[...]
    e = jnp.exp(x - jnp.max(x, axis=-1, keepdims=True))
    predicted = e * (1.0 / jnp.sum(e, axis=-1, keepdims=True))
    frame = first + lax.broadcasted_iota(jnp.int32, (R, 1), 0)
    valid = jnp.where(frame < s_len, 16.0, 0.0)
    total = jnp.sum(targets, axis=-1, keepdims=True)
    lgrad[...] = (valid * (total * predicted - targets)).astype(BF16)

    def s_hidden_grad(i):
        at = cols(i, 256)
        hid[:, at] = mm(lgrad[...], ws[at, pl.ds(DS, VOCAB)], NT).astype(BF16)

    project(0, DS // 256, s_hidden_grad)

    def s_mix_grad(i):
        at = cols(i, CW)
        qm[1, pl.ds(0, R), at] = mm(hid[:, pl.ds(0, DS)], ws[at, pl.ds(0, DS)], NT).astype(BF16)
        mc.start(i)

    project(0, DS // CW, s_mix_grad)

    def inner_pair(j, carry):
        at = cols(j, 128)
        prod = qm[1, pl.ds(0, R), at].astype(F32) * mix_s[:, at]
        zero = jnp.zeros_like(prod)
        in0 = jnp.sum(jnp.where(low, prod, zero), axis=-1, keepdims=True)
        in1 = jnp.sum(jnp.where(low, zero, prod), axis=-1, keepdims=True)
        st = stat_c[...]
        st = jnp.where(lane == 16 + 2 * j, in0, st)
        stat_c[...] = jnp.where(lane == 17 + 2 * j, in1, st)
        return carry

    lax.fori_loop(0, SP, inner_pair, 0)
    stat[:, pl.ds(0, R)] = stat_c[...].T[:32]
    sc.start(0)

    def query_pair(j):
        at = cols(j, 128)
        kat = cols(TP + j, 128)
        m = qm[1, pl.ds(0, R), at]
        dp = mm(stacked(m), kv[1, :, kat], NT).reshape(2, R, WIN)
        st = stat_c[...]
        zero = jnp.zeros_like(st)
        in0 = jnp.sum(jnp.where(lane == 16 + 2 * j, st, zero), axis=-1, keepdims=True)
        in1 = jnp.sum(jnp.where(lane == 17 + 2 * j, st, zero), axis=-1, keepdims=True)
        inner = jnp.concatenate([in0[None], in1[None]], axis=0)
        ds = (probs[j] * (dp - inner)).astype(BF16).reshape(2 * R, WIN)
        gq[0, :, at] = (merged(mm(ds, kv[0, :, kat])) * 0.125).astype(BF16)

    def query_chunk(c, carry):
        for i in range(PPC):
            query_pair(c * PPC + i)
        mc.a(c)

        @pl.when(c == 0)
        def _():
            sc.a(0)

        @pl.when(c == 1)
        def _():
            sc.b(0)

        @pl.when(c > 0)
        def _():
            mc.b(c - 1)

        return carry

    lax.fori_loop(0, SCH, query_chunk, 0)
    mc.b(SCH - 1)
    qc.c(0)
    sc.c(0)

    def key_pair(j):
        at = cols(j, 128)
        kat = cols(TP + j, 128)
        q = qm[0, :, at]
        m = qm[1, :, at]
        x = scores(kv[0, pl.ds(CTX, R), kat], q, bias_k[...])
        lse = jnp.concatenate([stat[pl.ds(2 * j, 1), :][None], stat[pl.ds(2 * j + 1, 1), :][None]], 0)
        inner = jnp.concatenate(
            [stat[pl.ds(16 + 2 * j, 1), :][None], stat[pl.ds(17 + 2 * j, 1), :][None]], 0
        )
        pr = jnp.exp(x - lse)
        gv[0, :, at] = merged(mm(pr.astype(BF16).reshape(2 * R, WIN), m)).astype(BF16)
        dp = mm(stacked(kv[1, pl.ds(CTX, R), kat]), m, NT).reshape(2, R, WIN)
        ds = (pr * (dp - inner)).astype(BF16).reshape(2 * R, WIN)
        gk[0, :, at] = (merged(mm(ds, q)) * 0.125).astype(BF16)

    def key_chunk(c, carry):
        mc.c(c)
        for i in range(PPC):
            key_pair(c * PPC + i)
        return carry

    lax.fori_loop(0, SCH, key_chunk, 0)

    def kv_sent(c, carry):
        kvc.sent(c)
        return carry

    lax.fori_loop(0, NCH, kv_sent, 0)

    def m_sent(c, carry):
        mc.sent(c)
        return carry

    lax.fori_loop(0, SCH, m_sent, 0)
    qc.sent(0)
    sc.sent(0)
    to_body.wait_send()
    to_tail.wait_send()
    for i in range(4):
        across(i).wait_send()
    for of in range(3):
        for kind in range(4):
            along(kind, of).wait_send()
        for step in range(NY):
            other_core(step, of).wait_send()


def on_device(*args):
    ns = lax.axis_size("seq")
    args = list(args)
    args[6] = args[6].reshape(1, VOCAB)
    args[13] = args[13].reshape(1, VOCAB)
    hbm = pl.BlockSpec(memory_space=pl.ANY)
    vmem = pl.BlockSpec(memory_space=pltpu.VMEM)
    smem = pl.BlockSpec(memory_space=pltpu.SMEM)
    in_specs = [hbm] * 16
    in_specs[6] = vmem
    in_specs[13] = vmem
    in_specs[14] = smem
    in_specs[15] = vmem
    out = jax.ShapeDtypeStruct((1, R, DS), BF16)
    dma = pltpu.SemaphoreType.DMA
    return pl.pallas_call(
        functools.partial(kernel, ns),
        out_shape=(out, out, out),
        in_specs=in_specs,
        out_specs=(vmem, vmem, vmem),
        scratch_shapes=[
            pltpu.VMEM((2, WIN, DT + DS), BF16),
            pltpu.VMEM((R, DT), BF16),
            pltpu.VMEM((R, DT), BF16),
            pltpu.VMEM((R, DS), BF16),
            pltpu.VMEM((DT, DT + VOCAB), BF16),
            pltpu.VMEM((DS, DS + VOCAB), BF16),
            pltpu.VMEM((2, WIN, DS), BF16),
            pltpu.VMEM((SP, 2, R, WIN), F32),
            pltpu.VMEM((R, DT), BF16),
            pltpu.VMEM((R, DS), BF16),
            pltpu.VMEM((R, DS), F32),
            pltpu.VMEM((R, DT), BF16),
            pltpu.VMEM((R, VOCAB), F32),
            pltpu.VMEM((R, VOCAB), BF16),
            pltpu.VMEM((R, VOCAB), BF16),
            pltpu.VMEM((R, VOCAB), BF16),
            pltpu.VMEM((R, VOCAB), BF16),
            pltpu.VMEM((R, WIN), F32),
            pltpu.VMEM((R, WIN), F32),
            pltpu.VMEM((R, WIN), F32),
            pltpu.VMEM((R, 128), F32),
            pltpu.VMEM((32, WIN), F32),
            dma((12,)),
            dma((4, NCH)),
            dma((4, NCH)),
            dma((4, 1)),
            dma((4, 1)),
            dma((4, SCH)),
            dma((4, SCH)),
            dma((4, 1)),
            dma((4, 1)),
            dma((4,)),
            dma((4,)),
            dma((4, 3)),
            dma((4, 3)),
            dma((4, 3)),
            dma((4, 3)),
            dma((2,)),
            dma((2,)),
        ],
        compiler_params=pltpu.CompilerParams(
            collective_id=0, has_side_effects=True, vmem_limit_bytes=56 * 1024 * 1024
        ),
    )(*args)


def solution(mesh):
    return jax.shard_map(
        on_device,
        mesh=mesh,
        in_specs=(
            P("grp", "seq", None),
            P("grp", "seq", None),
            P("grp", "seq", None),
            P("grp", "seq", None),
            P("grp", None),
            P("grp", None),
            P(),
            P("grp", "seq", None),
            P("grp", "seq", None),
            P("grp", "seq", None),
            P("grp", "seq", None),
            P("grp", None),
            P("grp", None),
            P(),
            P(),
            P("grp", "seq"),
        ),
        out_specs=(P("grp", "seq", None), P("grp", "seq", None), P("grp", "seq", None)),
        check_vma=False,
    )
```

```python
import functools

import jax
import jax.numpy as jnp
from jax import lax
from jax.experimental import pallas as pl
from jax.experimental.pallas import tpu as pltpu
from jax.sharding import PartitionSpec as P

CTX = 512
MAXD = 16
R = 128
WIN = CTX + R
DT = 1536
DS = 1024
VOCAB = 1024
TP = DT // 128
SP = DS // 128
CW = 128
TCH = DT // CW
SCH = DS // CW
NCH = TCH + SCH
NY = 4

FILL = -1e30
F32 = jnp.float32
BF16 = jnp.bfloat16
MESH = pl.DeviceIdType.MESH
NT = (((1,), (1,)), ((), ()))
NN = (((1,), (0,)), ((), ()))


def mm(a, b, dims=NN):
    return lax.dot_general(a, b, dims, preferred_element_type=F32)


def cols(i, width):
    return pl.ds(pl.multiple_of(i * width, width), width)


class Cast:
    def __init__(self, place, send, recv, group, seq, zdev, xdev, cdev, xl, core):
        self.place, self.send, self.recv = place, send, recv
        self.g, self.zdev, self.xdev, self.cdev = group, zdev, xdev, cdev
        self.xl, self.core = xl, core

    def copy(self, kind, chunk):
        if kind == 0:
            src, dst, dev = 0, 4, self.zdev
        elif kind == 1:
            src, dst, dev = 4 * self.xl, 2, self.xdev
        elif kind == 2:
            src, dst, dev = 4 * self.core, 1 + 2 * self.core, self.cdev
        else:
            src, dst, dev = 2, 3 - 2 * self.core, self.cdev
        return pltpu.make_async_remote_copy(
            src_ref=self.place(src, chunk),
            dst_ref=self.place(dst, chunk),
            send_sem=self.send.at[kind, chunk],
            recv_sem=self.recv.at[kind, chunk],
            device_id=(self.g, dev),
            device_id_type=MESH,
        )

    def start(self, chunk):
        self.copy(0, chunk).start()

    def landed(self, kind, chunk):
        dist = (4, 2, 3 - 2 * self.core, 1 + 2 * self.core)[kind]
        ref = self.place(dist, chunk)
        pltpu.make_async_remote_copy(
            src_ref=ref,
            dst_ref=ref,
            send_sem=self.send.at[kind, chunk],
            recv_sem=self.recv.at[kind, chunk],
            device_id=(self.g, self.cdev),
            device_id_type=MESH,
        ).wait_recv()

    def a(self, chunk):
        self.landed(0, chunk)
        self.copy(1, chunk).start()
        self.copy(2, chunk).start()

    def b(self, chunk):
        self.landed(1, chunk)
        self.copy(3, chunk).start()

    def c(self, chunk):
        self.landed(2, chunk)
        self.landed(3, chunk)

    def sent(self, chunk):
        for kind in range(4):
            self.copy(kind, chunk).wait_send()


def kernel(
    ns,
    tq,
    tk,
    tv,
    tr,
    tow,
    thw,
    thb,
    sq,
    sk,
    sv,
    sr,
    sow,
    shw,
    shb,
    lens,
    align,
    out,
    grads,
    kv,
    qt,
    rt,
    rs,
    wt,
    ws,
    qm,
    probs,
    ctx_t,
    ctx_s,
    mix_s,
    hid,
    logits,
    post,
    ext,
    tail,
    tail_in,
    lgrad,
    bias_t,
    bias_s,
    bias_k,
    stat_c,
    stat,
    lsem,
    osem,
    kv_send,
    kv_recv,
    q_send,
    q_recv,
    m_send,
    m_recv,
    s_send,
    s_recv,
    wx_send,
    wx_recv,
    wy_send,
    wy_recv,
    wc_send,
    wc_recv,
    p_send,
    p_recv,
):
    g = lax.axis_index("grp")
    s = lax.axis_index("seq")
    og = 1 - g
    core = lax.rem(s, 2)
    xl = lax.rem(s // 2, 2)
    ystep = ns // NY
    y = s // ystep
    xdev = s + 2 - 4 * xl
    cdev = s + 1 - 2 * core
    ahead = lax.rem(s + 4, ns)
    behind = lax.rem(s + ns - 4, ns)
    ynext = lax.rem(s + ystep, ns)
    yprev = lax.rem(s + ns - ystep, ns)
    s_next = lax.rem(s + 1, ns)
    s_prev = lax.rem(s + ns - 1, ns)
    inside = s - y * ystep
    znext = y * ystep + lax.rem(inside + 4, ystep)
    zprev = y * ystep + lax.rem(inside + ystep - 4, ystep)
    yp = lax.rem(y, 2)
    zp = lax.rem(inside // 4, 2)

    own = [
        (tk.at[0], kv.at[0, pl.ds(CTX, R), pl.ds(0, DT)]),
        (tv.at[0], kv.at[1, pl.ds(CTX, R), pl.ds(0, DT)]),
        (sk.at[0], kv.at[0, pl.ds(CTX, R), pl.ds(DT, DS)]),
        (sv.at[0], kv.at[1, pl.ds(CTX, R), pl.ds(DT, DS)]),
        (sq.at[0], qm.at[0, pl.ds(0, R), :]),
        (tq.at[0], qt),
        (tr.at[0], rt),
        (sr.at[0], rs),
        (tow, wt.at[pl.ds(pl.multiple_of(g * (DT // 2), DT // 2), DT // 2), pl.ds(0, DT)]),
        (thw, wt.at[pl.ds(pl.multiple_of(g * (DT // 2), DT // 2), DT // 2), pl.ds(DT, VOCAB)]),
        (sow, ws.at[pl.ds(pl.multiple_of(g * (DS // 2), DS // 2), DS // 2), pl.ds(0, DS)]),
        (shw, ws.at[pl.ds(pl.multiple_of(g * (DS // 2), DS // 2), DS // 2), pl.ds(DS, VOCAB)]),
    ]
    local = [pltpu.make_async_copy(a, b, lsem.at[i]) for i, (a, b) in enumerate(own)]
    for item in local:
        item.start()
    tail[pl.ds(MAXD, R - MAXD), :] = jnp.zeros((R - MAXD, VOCAB), BF16)

    barrier = pltpu.get_barrier_semaphore()
    peers = [
        (g, xdev),
        (g, cdev),
        (g, ahead),
        (g, behind),
        (g, ynext),
        (g, yprev),
        (g, znext),
        (g, zprev),
        (og, xdev),
        (og, s),
        (g, s_next),
        (g, s_prev),
    ]
    for peer in peers:
        pl.semaphore_signal(barrier, inc=1, device_id=peer, device_id_type=MESH)

    row = lax.broadcasted_iota(jnp.int32, (R, WIN), 0)
    col = lax.broadcasted_iota(jnp.int32, (R, WIN), 1)
    band = (col >= row) & (col <= row + CTX)
    first = s * R
    t_len = lens[g]
    s_len = lens[og]
    key_pos = first - CTX + col
    seen = band & (key_pos >= 0)
    bias_t[...] = jnp.where(seen & (key_pos < t_len), 0.0, FILL)
    bias_s[...] = jnp.where(seen & (key_pos < s_len), 0.0, FILL)
    bias_k[...] = jnp.where(band & (first + col < ns * R) & (first + row < s_len), 0.0, FILL)
    stat_c[...] = jnp.zeros_like(stat_c)

    pl.semaphore_wait(barrier, len(peers))

    def kv_place(dist, chunk):
        return kv.at[:, cols(4 - dist, R), cols(chunk, CW)]

    def q_place(dist, chunk):
        return qm.at[0, cols(dist, R), :]

    def m_place(dist, chunk):
        return qm.at[1, cols(dist, R), cols(chunk, CW)]

    def s_place(dist, chunk):
        return stat.at[:, cols(dist, R)]

    kvc = Cast(kv_place, kv_send, kv_recv, g, s, ahead, xdev, cdev, xl, core)
    back = (g, s, behind, xdev, cdev, 1 - xl, 1 - core)
    qc = Cast(q_place, q_send, q_recv, *back)
    mc = Cast(m_place, m_send, m_recv, *back)
    sc = Cast(s_place, s_send, s_recv, *back)

    def piece_rows(k, ypar, zpar):
        if k < 4:
            n = DT // 32
            return (((ypar * 2 + zpar) * 2 + core) * 2 + k % 2) * n, n
        n = DS // 8
        return ((ypar, zpar)[k - 4] * 2 + core) * n, n

    def piece(group, k, ypar, zpar):
        first, n = piece_rows(k, ypar, zpar)
        half = DT // 2 if k < 4 else DS // 2
        rows = pl.ds(pl.multiple_of(group * half + first, 16), n)
        if k < 4:
            return wt.at[rows, (pl.ds(0, DT), pl.ds(DT, VOCAB))[k // 2]]
        return ws.at[rows, (pl.ds(0, DS), pl.ds(DS, VOCAB))[k - 4]]

    def across(k):
        first, n = piece_rows(k, yp, zp)
        source = (tow, tow, thw, thw, sow, shw)[k]
        return pltpu.make_async_remote_copy(
            src_ref=source.at[pl.ds(pl.multiple_of(first, 16), n), :],
            dst_ref=piece(g, k, yp, zp),
            send_sem=wx_send.at[k],
            recv_sem=wx_recv.at[k],
            device_id=(og, xdev),
            device_id_type=MESH,
        )

    def along(k, kind):
        if kind < 2:
            ref, dev = piece(og, k, yp, zp), (yprev, zprev)[kind]
        elif k % 2 == 0:
            ref, dev = piece(og, k, yp, 1 - zp), yprev
        else:
            ref, dev = piece(og, k, 1 - yp, zp), zprev
        return pltpu.make_async_remote_copy(
            src_ref=ref,
            dst_ref=ref,
            send_sem=wy_send.at[kind, k],
            recv_sem=wy_recv.at[kind, k],
            device_id=(g, dev),
            device_id_type=MESH,
        )

    def kinds(k):
        return (0, 1) if k < 4 else (k - 4,)

    def other_core(k, which):
        ypar = 1 - yp if which in (1, 3) else yp
        zpar = 1 - zp if which in (2, 3) else zp
        ref = piece(og, k, ypar, zpar)
        return pltpu.make_async_remote_copy(
            src_ref=ref,
            dst_ref=ref,
            send_sem=wc_send.at[which, k],
            recv_sem=wc_recv.at[which, k],
            device_id=(g, cdev),
            device_id_type=MESH,
        )

    def pieces(k):
        return (0, 1, 2, 3) if k < 4 else (0, k - 3)

    def w_first(k):
        across(k).wait_recv()
        for kind in kinds(k):
            along(k, kind).start()
        other_core(k, 0).start()

    def w_second(k):
        for kind in kinds(k):
            along(k, kind).wait_recv()
        if k < 4:
            along(k, 2).start()
        for kind in kinds(k):
            other_core(k, 1 + kind).start()

    def w_third(k):
        along(k, 2).wait_recv()
        other_core(k, 3).start()

    def w_ready(k):
        for which in pieces(k):
            other_core(k, which).wait_recv()

    for k in range(6):
        across(k).start()
    local[0].wait()
    local[1].wait()
    for c in range(TCH):
        kvc.start(c)
    local[2].wait()
    local[3].wait()
    for c in range(TCH, NCH):
        kvc.start(c)
    for item in local[4:]:
        item.wait()

    lane = lax.broadcasted_iota(jnp.int32, (R, 128), 1)
    low = lane < 64

    def stacked(x):
        zero = jnp.zeros_like(x)
        return jnp.concatenate([jnp.where(low, x, zero), jnp.where(low, zero, x)], axis=0)

    def merged(x):
        return jnp.where(low, x[:R], x[R:])

    def scores(q, k, bias):
        sc2 = mm(stacked(q * 0.125), k, NT)
        return sc2.reshape(2, R, WIN) + bias[None]

    def teacher_pair(p):
        at = cols(p, 128)
        x = scores(qt[:, at], kv[0, :, at], bias_t[...])
        top = jnp.max(x, axis=-1, keepdims=True)
        e = jnp.exp(x - top)
        inv = 1.0 / jnp.sum(e, axis=-1, keepdims=True)
        o = mm(e.astype(BF16).reshape(2 * R, WIN), kv[1, :, at])
        o = o * inv.reshape(2 * R, 1)
        ctx_t[:, at] = merged(o).astype(BF16)

    def project(lo, hi, fn):
        def body(i, carry):
            fn(i)
            return carry

        lax.fori_loop(lo, hi, body, 0)

    kvc.a(0)

    def at_step(i, steps):
        for step, calls in steps.items():

            @pl.when(i == step)
            def _():
                for call, k in calls:
                    call(k)

    def teacher_chunk(i, carry):
        at_step(
            i,
            {
                1: [(w_first, 0)],
                3: [(w_first, 1), (w_second, 0)],
                4: [(w_first, 2)],
                6: [(w_first, 3), (w_second, 1)],
                8: [(w_third, 0)],
                10: [(w_second, 2), (w_third, 1), (w_first, 4)],
                11: [(w_second, 3)],
            },
        )
        kvc.a(i + 1)

        @pl.when(i >= 1)
        def _():
            kvc.b(i - 1)

        @pl.when(i >= 2)
        def _():
            kvc.c(i - 2)
            teacher_pair(i - 2)

        return carry

    lax.fori_loop(0, TCH, teacher_chunk, 0)

    def teacher_last(i, carry):
        at_step(i, {TCH + 1: [(w_third, 2), (w_third, 3)]})
        kvc.a(i + 1)
        kvc.b(i - 1)
        kvc.c(i - 2)
        teacher_pair(i - 2)
        return carry

    lax.fori_loop(TCH, TCH + 2, teacher_last, 0)

    def t_hidden(i):
        at = cols(i, 256)
        hid[:, at] = (rt[:, at].astype(F32) + mm(ctx_t[...], wt[:, at])).astype(BF16)

    def t_logits(i):
        at = cols(i, 256)
        logits[:, at] = mm(hid[...], wt[:, pl.ds(pl.multiple_of(DT + i * 256, 256), 256)]) + thb[:, at]

    def student_pair(j):
        at = cols(TP + j, 128)
        x = scores(qm[0, pl.ds(0, R), cols(j, 128)], kv[0, :, at], bias_s[...])
        top = jnp.max(x, axis=-1, keepdims=True)
        e = jnp.exp(x - top)
        total = jnp.sum(e, axis=-1, keepdims=True)
        pr = e * (1.0 / total)
        probs[j] = pr
        o = mm(pr.astype(BF16).reshape(2 * R, WIN), kv[1, :, at])
        o = merged(o)
        mix_s[:, cols(j, 128)] = o
        ctx_s[:, cols(j, 128)] = o.astype(BF16)
        lse = top + jnp.log(total)
        st = stat_c[...]
        st = jnp.where(lane == 2 * j, lse[0], st)
        stat_c[...] = jnp.where(lane == 2 * j + 1, lse[1], st)

    def student_pairs(lo, hi):
        def body(j, carry):
            kvc.c(TCH + j)
            student_pair(j)
            return carry

        lax.fori_loop(lo, hi, body, 0)

    w_first(5)
    kvc.a(TCH + 3)
    kvc.b(TCH + 1)
    w_ready(0)
    w_ready(1)
    project(0, 4, t_hidden)
    kvc.a(TCH + 4)
    kvc.b(TCH + 2)
    project(4, DT // 256, t_hidden)
    w_ready(2)
    w_ready(3)
    project(0, 2, t_logits)
    kvc.a(TCH + 5)
    kvc.b(TCH + 3)
    project(2, VOCAB // 256, t_logits)
    x = logits[...]
    e = jnp.exp(x - jnp.max(x, axis=-1, keepdims=True))
    post[...] = (e * (1.0 / jnp.sum(e, axis=-1, keepdims=True))).astype(BF16)
    to_body = pltpu.make_async_remote_copy(
        src_ref=post,
        dst_ref=ext,
        send_sem=p_send.at[0],
        recv_sem=p_recv.at[0],
        device_id=(og, s),
        device_id_type=MESH,
    )
    to_next = pltpu.make_async_remote_copy(
        src_ref=post.at[pl.ds(R - MAXD, MAXD), :],
        dst_ref=tail_in,
        send_sem=p_send.at[1],
        recv_sem=p_recv.at[1],
        device_id=(g, s_next),
        device_id_type=MESH,
    )
    to_tail = pltpu.make_async_remote_copy(
        src_ref=tail_in,
        dst_ref=tail.at[pl.ds(0, MAXD), :],
        send_sem=p_send.at[2],
        recv_sem=p_recv.at[2],
        device_id=(og, s),
        device_id_type=MESH,
    )
    to_next.start()
    to_body.start()

    qc.start(0)
    kvc.a(TCH + 6)
    kvc.b(TCH + 4)
    student_pairs(0, 2)
    to_next.wait_recv()
    to_tail.start()
    w_second(4)
    kvc.a(TCH + 7)
    kvc.b(TCH + 5)
    student_pairs(2, 4)
    kvc.b(TCH + 6)
    student_pairs(4, 5)
    w_second(5)
    kvc.b(TCH + 7)
    student_pairs(5, 6)
    qc.a(0)
    student_pairs(6, 8)
    w_ready(4)

    def s_hidden(i):
        at = cols(i, 256)
        hid[:, at] = (rs[:, at].astype(F32) + mm(ctx_s[...], ws[:, at])).astype(BF16)

    project(0, DS // 256, s_hidden)
    w_ready(5)

    def s_logits(i):
        at = cols(i, 256)
        w = ws[:, pl.ds(pl.multiple_of(DS + i * 256, 256), 256)]
        logits[:, at] = mm(hid[:, pl.ds(0, DS)], w) + shb[:, at]

    project(0, VOCAB // 256, s_logits)

    rows = jnp.broadcast_to(align[...], (R, R)).T - first
    pick_body = jnp.where(rows == lane, 1.0, 0.0).astype(BF16)
    pick_tail = jnp.where(rows + MAXD == lane, 1.0, 0.0)
    pick_tail = jnp.where(lane < MAXD, pick_tail, 0.0).astype(BF16)
    to_body.wait_recv()
    to_tail.wait_recv()
    targets = mm(pick_body, ext[...]) + mm(pick_tail, tail[...])
    x = logits[...]
    e = jnp.exp(x - jnp.max(x, axis=-1, keepdims=True))
    predicted = e * (1.0 / jnp.sum(e, axis=-1, keepdims=True))
    frame = first + lax.broadcasted_iota(jnp.int32, (R, 1), 0)
    valid = jnp.where(frame < s_len, 16.0, 0.0)
    total = jnp.sum(targets, axis=-1, keepdims=True)
    lgrad[...] = (valid * (total * predicted - targets)).astype(BF16)

    def s_hidden_grad(i):
        at = cols(i, 256)
        hid[:, at] = mm(lgrad[...], ws[at, pl.ds(DS, VOCAB)], NT).astype(BF16)

    project(0, DS // 256, s_hidden_grad)

    def s_mix_grad(i):
        at = cols(i, 256)
        qm[1, pl.ds(0, R), at] = mm(hid[:, pl.ds(0, DS)], ws[at, pl.ds(0, DS)], NT).astype(BF16)
        mc.start(2 * i)
        mc.start(2 * i + 1)

    project(0, DS // 256, s_mix_grad)

    def inner_pair(j, carry):
        at = cols(j, 128)
        prod = qm[1, pl.ds(0, R), at].astype(F32) * mix_s[:, at]
        zero = jnp.zeros_like(prod)
        in0 = jnp.sum(jnp.where(low, prod, zero), axis=-1, keepdims=True)
        in1 = jnp.sum(jnp.where(low, zero, prod), axis=-1, keepdims=True)
        st = stat_c[...]
        st = jnp.where(lane == 16 + 2 * j, in0, st)
        stat_c[...] = jnp.where(lane == 17 + 2 * j, in1, st)
        return carry

    qc.b(0)
    lax.fori_loop(0, SP, inner_pair, 0)
    stat[:, pl.ds(0, R)] = stat_c[...].T[:32]
    sc.start(0)

    def query_pair(j):
        at = cols(j, 128)
        kat = cols(TP + j, 128)
        m = qm[1, pl.ds(0, R), at]
        dp = mm(stacked(m), kv[1, :, kat], NT).reshape(2, R, WIN)
        st = stat_c[...]
        zero = jnp.zeros_like(st)
        in0 = jnp.sum(jnp.where(lane == 16 + 2 * j, st, zero), axis=-1, keepdims=True)
        in1 = jnp.sum(jnp.where(lane == 17 + 2 * j, st, zero), axis=-1, keepdims=True)
        inner = jnp.concatenate([in0[None], in1[None]], axis=0)
        ds = (probs[j] * (dp - inner)).astype(BF16).reshape(2 * R, WIN)
        grads[0, :, at] = (merged(mm(ds, kv[0, :, kat])) * 0.125).astype(BF16)

    def key_pair(j):
        at = cols(j, 128)
        kat = cols(TP + j, 128)
        q = qm[0, :, at]
        m = qm[1, :, at]
        x = scores(kv[0, pl.ds(CTX, R), kat], q, bias_k[...])
        lse = jnp.concatenate([stat[pl.ds(2 * j, 1), :][None], stat[pl.ds(2 * j + 1, 1), :][None]], 0)
        inner = jnp.concatenate(
            [stat[pl.ds(16 + 2 * j, 1), :][None], stat[pl.ds(17 + 2 * j, 1), :][None]], 0
        )
        pr = jnp.exp(x - lse)
        grads[2, :, at] = merged(mm(pr.astype(BF16).reshape(2 * R, WIN), m)).astype(BF16)
        dp = mm(stacked(kv[1, pl.ds(CTX, R), kat]), m, NT).reshape(2, R, WIN)
        ds = (pr * (dp - inner)).astype(BF16).reshape(2 * R, WIN)
        grads[1, :, at] = (merged(mm(ds, q)) * 0.125).astype(BF16)

    def result(i, j):
        at = cols(j, 128)
        return pltpu.make_async_copy(grads.at[i, :, at], out.at[i, :, at], osem.at[i, j])

    def key_step(j):
        mc.c(j)
        key_pair(j)
        result(1, j).start()
        result(2, j).start()

    def last_chunk(i, carry):
        query_pair(i)
        result(0, i).start()
        mc.a(i)

        @pl.when(i == 1)
        def _():
            sc.a(0)

        @pl.when(i >= 3)
        def _():
            mc.b(i - 3)

        @pl.when(i == 4)
        def _():
            sc.b(0)
            qc.c(0)

        @pl.when(i == 5)
        def _():
            sc.c(0)

        @pl.when(i >= 5)
        def _():
            key_step(i - 5)

        return carry

    lax.fori_loop(0, SP, last_chunk, 0)

    def rest(i, carry):
        @pl.when(i < 6)
        def _():
            mc.b(i + 2)

        key_step(i)
        return carry

    lax.fori_loop(3, SP, rest, 0)

    def kv_sent(c, carry):
        kvc.sent(c)
        return carry

    lax.fori_loop(0, NCH, kv_sent, 0)

    def m_sent(c, carry):
        mc.sent(c)
        return carry

    lax.fori_loop(0, SCH, m_sent, 0)
    def results(j, carry):
        for i in range(3):
            result(i, j).wait()
        return carry

    lax.fori_loop(0, SP, results, 0)
    qc.sent(0)
    sc.sent(0)
    to_body.wait_send()
    to_next.wait_send()
    to_tail.wait_send()
    for k in range(6):
        across(k).wait_send()
        for kind in (0, 1, 2) if k < 4 else kinds(k):
            along(k, kind).wait_send()
        for which in pieces(k):
            other_core(k, which).wait_send()


def on_device(*args):
    ns = lax.axis_size("seq")
    args = list(args)
    args[6] = args[6].reshape(1, VOCAB)
    args[13] = args[13].reshape(1, VOCAB)
    hbm = pl.BlockSpec(memory_space=pl.ANY)
    vmem = pl.BlockSpec(memory_space=pltpu.VMEM)
    smem = pl.BlockSpec(memory_space=pltpu.SMEM)
    in_specs = [hbm] * 16
    in_specs[6] = vmem
    in_specs[13] = vmem
    in_specs[14] = smem
    in_specs[15] = vmem
    out = jax.ShapeDtypeStruct((3, R, DS), BF16)
    dma = pltpu.SemaphoreType.DMA
    grads = pl.pallas_call(
        functools.partial(kernel, ns),
        out_shape=out,
        in_specs=in_specs,
        out_specs=hbm,
        scratch_shapes=[
            pltpu.VMEM((3, R, DS), BF16),
            pltpu.VMEM((2, WIN, DT + DS), BF16),
            pltpu.VMEM((R, DT), BF16),
            pltpu.VMEM((R, DT), BF16),
            pltpu.VMEM((R, DS), BF16),
            pltpu.VMEM((DT, DT + VOCAB), BF16),
            pltpu.VMEM((DS, DS + VOCAB), BF16),
            pltpu.VMEM((2, WIN, DS), BF16),
            pltpu.VMEM((SP, 2, R, WIN), F32),
            pltpu.VMEM((R, DT), BF16),
            pltpu.VMEM((R, DS), BF16),
            pltpu.VMEM((R, DS), F32),
            pltpu.VMEM((R, DT), BF16),
            pltpu.VMEM((R, VOCAB), F32),
            pltpu.VMEM((R, VOCAB), BF16),
            pltpu.VMEM((R, VOCAB), BF16),
            pltpu.VMEM((R, VOCAB), BF16),
            pltpu.VMEM((MAXD, VOCAB), BF16),
            pltpu.VMEM((R, VOCAB), BF16),
            pltpu.VMEM((R, WIN), F32),
            pltpu.VMEM((R, WIN), F32),
            pltpu.VMEM((R, WIN), F32),
            pltpu.VMEM((R, 128), F32),
            pltpu.VMEM((32, WIN), F32),
            dma((12,)),
            dma((3, SP)),
            dma((4, NCH)),
            dma((4, NCH)),
            dma((4, 1)),
            dma((4, 1)),
            dma((4, SCH)),
            dma((4, SCH)),
            dma((4, 1)),
            dma((4, 1)),
            dma((6,)),
            dma((6,)),
            dma((3, 6)),
            dma((3, 6)),
            dma((4, 6)),
            dma((4, 6)),
            dma((3,)),
            dma((3,)),
        ],
        compiler_params=pltpu.CompilerParams(
            collective_id=0, has_side_effects=True, vmem_limit_bytes=56 * 1024 * 1024
        ),
    )(*args)
    return grads[0:1], grads[1:2], grads[2:3]


def solution(mesh):
    return jax.shard_map(
        on_device,
        mesh=mesh,
        in_specs=(
            P("grp", "seq", None),
            P("grp", "seq", None),
            P("grp", "seq", None),
            P("grp", "seq", None),
            P("grp", None),
            P("grp", None),
            P(),
            P("grp", "seq", None),
            P("grp", "seq", None),
            P("grp", "seq", None),
            P("grp", "seq", None),
            P("grp", None),
            P("grp", None),
            P(),
            P(),
            P("grp", "seq"),
        ),
        out_specs=(P("grp", "seq", None), P("grp", "seq", None), P("grp", "seq", None)),
        check_vma=False,
    )
```

```python
import functools

import jax
import jax.numpy as jnp
from jax import lax
from jax.experimental import pallas as pl
from jax.experimental.pallas import tpu as pltpu
from jax.sharding import PartitionSpec as P

CTX = 512
MAXD = 16
R = 128
WIN = CTX + R
DT = 1536
DS = 1024
VOCAB = 1024
TP = DT // 128
SP = DS // 128
CW = 128
TCH = DT // CW
SCH = DS // CW
NCH = TCH + SCH
NY = 4

FILL = -1e30
F32 = jnp.float32
BF16 = jnp.bfloat16
MESH = pl.DeviceIdType.MESH
NT = (((1,), (1,)), ((), ()))
NN = (((1,), (0,)), ((), ()))


def mm(a, b, dims=NN):
    return lax.dot_general(a, b, dims, preferred_element_type=F32)


def cols(i, width):
    return pl.ds(pl.multiple_of(i * width, width), width)


class Cast:
    def __init__(self, place, send, recv, group, seq, zdev, xdev, cdev, xl, core):
        self.place, self.send, self.recv = place, send, recv
        self.g, self.zdev, self.xdev, self.cdev = group, zdev, xdev, cdev
        self.xl, self.core = xl, core

    def copy(self, kind, chunk):
        if kind == 0:
            src, dst, dev = 0, 4, self.zdev
        elif kind == 1:
            src, dst, dev = 4 * self.xl, 2, self.xdev
        elif kind == 2:
            src, dst, dev = 4 * self.core, 1 + 2 * self.core, self.cdev
        else:
            src, dst, dev = 2, 3 - 2 * self.core, self.cdev
        return pltpu.make_async_remote_copy(
            src_ref=self.place(src, chunk),
            dst_ref=self.place(dst, chunk),
            send_sem=self.send.at[kind, chunk],
            recv_sem=self.recv.at[kind, chunk],
            device_id=(self.g, dev),
            device_id_type=MESH,
        )

    def start(self, chunk):
        self.copy(0, chunk).start()

    def landed(self, kind, chunk):
        dist = (4, 2, 3 - 2 * self.core, 1 + 2 * self.core)[kind]
        ref = self.place(dist, chunk)
        pltpu.make_async_remote_copy(
            src_ref=ref,
            dst_ref=ref,
            send_sem=self.send.at[kind, chunk],
            recv_sem=self.recv.at[kind, chunk],
            device_id=(self.g, self.cdev),
            device_id_type=MESH,
        ).wait_recv()

    def a(self, chunk):
        self.landed(0, chunk)
        self.copy(1, chunk).start()
        self.copy(2, chunk).start()

    def b(self, chunk):
        self.landed(1, chunk)
        self.copy(3, chunk).start()

    def c(self, chunk):
        self.landed(2, chunk)
        self.landed(3, chunk)

    def sent(self, chunk):
        for kind in range(4):
            self.copy(kind, chunk).wait_send()


def kernel(
    ns,
    tq,
    tk,
    tv,
    tr,
    tow,
    thw,
    thb,
    sq,
    sk,
    sv,
    sr,
    sow,
    shw,
    shb,
    lens,
    align,
    out,
    grads,
    kv,
    qt,
    rt,
    rs,
    wt,
    ws,
    qm,
    probs,
    ctx_t,
    ctx_s,
    mix_s,
    hid,
    logits,
    post,
    ext,
    tail_in,
    lgrad,
    bias_t,
    bias_s,
    bias_k,
    stat_c,
    stat,
    lsem,
    osem,
    kv_send,
    kv_recv,
    q_send,
    q_recv,
    m_send,
    m_recv,
    s_send,
    s_recv,
    wx_send,
    wx_recv,
    wy_send,
    wy_recv,
    wc_send,
    wc_recv,
    p_send,
    p_recv,
):
    g = lax.axis_index("grp")
    s = lax.axis_index("seq")
    og = 1 - g
    core = lax.rem(s, 2)
    xl = lax.rem(s // 2, 2)
    ystep = ns // NY
    y = s // ystep
    xdev = s + 2 - 4 * xl
    cdev = s + 1 - 2 * core
    ahead = lax.rem(s + 4, ns)
    behind = lax.rem(s + ns - 4, ns)
    ynext = lax.rem(s + ystep, ns)
    yprev = lax.rem(s + ns - ystep, ns)
    s_next = lax.rem(s + 1, ns)
    s_prev = lax.rem(s + ns - 1, ns)
    inside = s - y * ystep
    znext = y * ystep + lax.rem(inside + 4, ystep)
    zprev = y * ystep + lax.rem(inside + ystep - 4, ystep)
    yp = lax.rem(y, 2)
    zp = lax.rem(inside // 4, 2)

    own = [
        (tk.at[0], kv.at[0, pl.ds(CTX, R), pl.ds(0, DT)]),
        (tv.at[0], kv.at[1, pl.ds(CTX, R), pl.ds(0, DT)]),
        (sk.at[0], kv.at[0, pl.ds(CTX, R), pl.ds(DT, DS)]),
        (sv.at[0], kv.at[1, pl.ds(CTX, R), pl.ds(DT, DS)]),
        (sq.at[0], qm.at[0, pl.ds(0, R), :]),
        (tq.at[0], qt),
        (tr.at[0], rt),
        (sr.at[0], rs),
        (tow, wt.at[pl.ds(pl.multiple_of(g * (DT // 2), DT // 2), DT // 2), pl.ds(0, DT)]),
        (thw, wt.at[pl.ds(pl.multiple_of(g * (DT // 2), DT // 2), DT // 2), pl.ds(DT, VOCAB)]),
        (sow, ws.at[pl.ds(pl.multiple_of(g * (DS // 2), DS // 2), DS // 2), pl.ds(0, DS)]),
        (shw, ws.at[pl.ds(pl.multiple_of(g * (DS // 2), DS // 2), DS // 2), pl.ds(DS, VOCAB)]),
    ]
    local = [pltpu.make_async_copy(a, b, lsem.at[i]) for i, (a, b) in enumerate(own)]
    for item in local:
        item.start()
    ext[pl.ds(R + MAXD, R - MAXD), :] = jnp.zeros((R - MAXD, VOCAB), BF16)

    barrier = pltpu.get_barrier_semaphore()
    peers = [
        (g, xdev),
        (g, cdev),
        (g, ahead),
        (g, behind),
        (g, ynext),
        (g, yprev),
        (g, znext),
        (g, zprev),
        (og, xdev),
        (og, s),
        (g, s_next),
        (g, s_prev),
    ]
    for peer in peers:
        pl.semaphore_signal(barrier, inc=1, device_id=peer, device_id_type=MESH)

    row = lax.broadcasted_iota(jnp.int32, (R, WIN), 0)
    col = lax.broadcasted_iota(jnp.int32, (R, WIN), 1)
    band = (col >= row) & (col <= row + CTX)
    first = s * R
    t_len = lens[g]
    s_len = lens[og]
    key_pos = first - CTX + col
    seen = band & (key_pos >= 0)
    bias_t[...] = jnp.where(seen & (key_pos < t_len), 0.0, FILL)
    bias_s[...] = jnp.where(seen & (key_pos < s_len), 0.0, FILL)
    bias_k[...] = jnp.where(band & (first + col < ns * R) & (first + row < s_len), 0.0, FILL)
    stat_c[...] = jnp.zeros_like(stat_c)

    pl.semaphore_wait(barrier, len(peers))

    def kv_place(dist, chunk):
        return kv.at[:, cols(4 - dist, R), cols(chunk, CW)]

    def q_place(dist, chunk):
        return qm.at[0, cols(dist, R), :]

    def m_place(dist, chunk):
        return qm.at[1, cols(dist, R), cols(chunk, CW)]

    def s_place(dist, chunk):
        return stat.at[:, cols(dist, R)]

    kvc = Cast(kv_place, kv_send, kv_recv, g, s, ahead, xdev, cdev, xl, core)
    back = (g, s, behind, xdev, cdev, 1 - xl, 1 - core)
    qc = Cast(q_place, q_send, q_recv, *back)
    mc = Cast(m_place, m_send, m_recv, *back)
    sc = Cast(s_place, s_send, s_recv, *back)

    def piece_rows(k, ypar, zpar):
        if k < 4:
            n = DT // 32
            return (((ypar * 2 + zpar) * 2 + core) * 2 + k % 2) * n, n
        n = DS // 8
        return ((ypar, zpar)[k - 4] * 2 + core) * n, n

    def piece(group, k, ypar, zpar):
        first, n = piece_rows(k, ypar, zpar)
        half = DT // 2 if k < 4 else DS // 2
        rows = pl.ds(pl.multiple_of(group * half + first, 16), n)
        if k < 4:
            return wt.at[rows, (pl.ds(0, DT), pl.ds(DT, VOCAB))[k // 2]]
        return ws.at[rows, (pl.ds(0, DS), pl.ds(DS, VOCAB))[k - 4]]

    def across(k):
        first, n = piece_rows(k, yp, zp)
        source = (tow, tow, thw, thw, sow, shw)[k]
        return pltpu.make_async_remote_copy(
            src_ref=source.at[pl.ds(pl.multiple_of(first, 16), n), :],
            dst_ref=piece(g, k, yp, zp),
            send_sem=wx_send.at[k],
            recv_sem=wx_recv.at[k],
            device_id=(og, xdev),
            device_id_type=MESH,
        )

    def along(k, kind):
        if kind < 2:
            ref, dev = piece(og, k, yp, zp), (yprev, zprev)[kind]
        elif k % 2 == 0:
            ref, dev = piece(og, k, yp, 1 - zp), yprev
        else:
            ref, dev = piece(og, k, 1 - yp, zp), zprev
        return pltpu.make_async_remote_copy(
            src_ref=ref,
            dst_ref=ref,
            send_sem=wy_send.at[kind, k],
            recv_sem=wy_recv.at[kind, k],
            device_id=(g, dev),
            device_id_type=MESH,
        )

    def kinds(k):
        return (0, 1) if k < 4 else (k - 4,)

    def other_core(k, which):
        ypar = 1 - yp if which in (1, 3) else yp
        zpar = 1 - zp if which in (2, 3) else zp
        ref = piece(og, k, ypar, zpar)
        return pltpu.make_async_remote_copy(
            src_ref=ref,
            dst_ref=ref,
            send_sem=wc_send.at[which, k],
            recv_sem=wc_recv.at[which, k],
            device_id=(g, cdev),
            device_id_type=MESH,
        )

    def pieces(k):
        return (0, 1, 2, 3) if k < 4 else (0, k - 3)

    def w_first(k):
        across(k).wait_recv()
        for kind in kinds(k):
            along(k, kind).start()
        other_core(k, 0).start()

    def w_second(k):
        for kind in kinds(k):
            along(k, kind).wait_recv()
        if k < 4:
            along(k, 2).start()
        for kind in kinds(k):
            other_core(k, 1 + kind).start()

    def w_third(k):
        along(k, 2).wait_recv()
        other_core(k, 3).start()

    def w_ready(k):
        for which in pieces(k):
            other_core(k, which).wait_recv()

    for k in range(6):
        across(k).start()
    local[0].wait()
    local[1].wait()
    for c in range(TCH):
        kvc.start(c)
    local[2].wait()
    local[3].wait()
    for c in range(TCH, NCH):
        kvc.start(c)
    for item in local[4:]:
        item.wait()

    lane = lax.broadcasted_iota(jnp.int32, (R, 128), 1)
    low = lane < 64

    def stacked(x):
        zero = jnp.zeros_like(x)
        return jnp.concatenate([jnp.where(low, x, zero), jnp.where(low, zero, x)], axis=0)

    def merged(x):
        return jnp.where(low, x[:R], x[R:])

    def scores(q, k, bias):
        sc2 = mm(stacked(q * 0.125), k, NT)
        return sc2.reshape(2, R, WIN) + bias[None]

    def teacher_pair(p):
        at = cols(p, 128)
        x = scores(qt[:, at], kv[0, :, at], bias_t[...])
        top = jnp.max(x, axis=-1, keepdims=True)
        e = jnp.exp(x - top)
        inv = 1.0 / jnp.sum(e, axis=-1, keepdims=True)
        o = mm(e.astype(BF16).reshape(2 * R, WIN), kv[1, :, at])
        o = o * inv.reshape(2 * R, 1)
        ctx_t[:, at] = merged(o).astype(BF16)

    def project(lo, hi, fn):
        def body(i, carry):
            fn(i)
            return carry

        lax.fori_loop(lo, hi, body, 0)

    kvc.a(0)

    def at_step(i, steps):
        for step, calls in steps.items():

            @pl.when(i == step)
            def _():
                for call, k in calls:
                    call(k)

    def teacher_chunk(i, carry):
        at_step(
            i,
            {
                1: [(w_first, 0)],
                3: [(w_first, 1), (w_second, 0)],
                4: [(w_first, 2)],
                6: [(w_first, 3), (w_second, 1)],
                8: [(w_third, 0)],
                10: [(w_second, 2), (w_third, 1), (w_first, 4)],
                11: [(w_second, 3)],
            },
        )
        kvc.a(i + 1)

        @pl.when(i >= 1)
        def _():
            kvc.b(i - 1)

        @pl.when(i >= 2)
        def _():
            kvc.c(i - 2)
            teacher_pair(i - 2)

        return carry

    lax.fori_loop(0, TCH, teacher_chunk, 0)

    def teacher_last(i, carry):
        at_step(i, {TCH + 1: [(w_third, 2), (w_third, 3)]})
        kvc.a(i + 1)
        kvc.b(i - 1)
        kvc.c(i - 2)
        teacher_pair(i - 2)
        return carry

    lax.fori_loop(TCH, TCH + 2, teacher_last, 0)

    def t_hidden(i):
        at = cols(i, 256)
        hid[:, at] = (rt[:, at].astype(F32) + mm(ctx_t[...], wt[:, at])).astype(BF16)

    def t_logits(i):
        at = cols(i, 256)
        logits[:, at] = mm(hid[...], wt[:, pl.ds(pl.multiple_of(DT + i * 256, 256), 256)]) + thb[:, at]

    def student_pair(j):
        at = cols(TP + j, 128)
        x = scores(qm[0, pl.ds(0, R), cols(j, 128)], kv[0, :, at], bias_s[...])
        top = jnp.max(x, axis=-1, keepdims=True)
        e = jnp.exp(x - top)
        total = jnp.sum(e, axis=-1, keepdims=True)
        pr = e * (1.0 / total)
        probs[j] = pr
        o = mm(pr.astype(BF16).reshape(2 * R, WIN), kv[1, :, at])
        o = merged(o)
        mix_s[:, cols(j, 128)] = o
        ctx_s[:, cols(j, 128)] = o.astype(BF16)
        lse = top + jnp.log(total)
        st = stat_c[...]
        st = jnp.where(lane == 2 * j, lse[0], st)
        stat_c[...] = jnp.where(lane == 2 * j + 1, lse[1], st)

    def student_pairs(lo, hi):
        for j in range(lo, hi):
            kvc.c(TCH + j)
        for j in range(lo, hi):
            student_pair(j)

    w_first(5)
    kvc.a(TCH + 3)
    kvc.b(TCH + 1)
    w_ready(0)
    w_ready(1)
    project(0, 4, t_hidden)
    kvc.a(TCH + 4)
    kvc.b(TCH + 2)
    project(4, DT // 256, t_hidden)
    w_ready(2)
    w_ready(3)
    project(0, 2, t_logits)
    kvc.a(TCH + 5)
    kvc.b(TCH + 3)
    project(2, VOCAB // 256, t_logits)
    x = logits[...]
    e = jnp.exp(x - jnp.max(x, axis=-1, keepdims=True))
    post[...] = (e * (1.0 / jnp.sum(e, axis=-1, keepdims=True))).astype(BF16)
    to_body = pltpu.make_async_remote_copy(
        src_ref=post,
        dst_ref=ext.at[pl.ds(0, R), :],
        send_sem=p_send.at[0],
        recv_sem=p_recv.at[0],
        device_id=(og, s),
        device_id_type=MESH,
    )
    to_next = pltpu.make_async_remote_copy(
        src_ref=post.at[pl.ds(R - MAXD, MAXD), :],
        dst_ref=tail_in,
        send_sem=p_send.at[1],
        recv_sem=p_recv.at[1],
        device_id=(g, s_next),
        device_id_type=MESH,
    )
    to_tail = pltpu.make_async_remote_copy(
        src_ref=tail_in,
        dst_ref=ext.at[pl.ds(R, MAXD), :],
        send_sem=p_send.at[2],
        recv_sem=p_recv.at[2],
        device_id=(og, s),
        device_id_type=MESH,
    )
    to_next.start()

    qc.start(0)
    kvc.a(TCH + 6)
    kvc.b(TCH + 4)
    student_pairs(0, 2)
    to_next.wait_recv()
    to_tail.start()
    w_second(4)
    kvc.a(TCH + 7)
    to_body.start()
    kvc.b(TCH + 5)
    student_pairs(2, 4)
    kvc.b(TCH + 6)
    student_pairs(4, 6)
    w_second(5)
    kvc.b(TCH + 7)
    student_pairs(6, 8)
    w_ready(4)

    def s_hidden(i):
        at = cols(i, 256)
        hid[:, at] = (rs[:, at].astype(F32) + mm(ctx_s[...], ws[:, at])).astype(BF16)

    project(0, DS // 256, s_hidden)
    w_ready(5)

    def s_logits(i):
        at = cols(i, 256)
        w = ws[:, pl.ds(pl.multiple_of(DS + i * 256, 256), 256)]
        logits[:, at] = mm(hid[:, pl.ds(0, DS)], w) + shb[:, at]

    project(0, VOCAB // 256, s_logits)

    rows = jnp.broadcast_to(align[...], (R, R)).T - first
    pick_body = jnp.where(rows == lane, 1.0, 0.0).astype(BF16)
    pick_tail = jnp.where(rows + MAXD == lane, 1.0, 0.0)
    pick_tail = jnp.where(lane < MAXD, pick_tail, 0.0).astype(BF16)
    pick = jnp.concatenate([pick_body, pick_tail], axis=1)
    x = logits[...]
    e = jnp.exp(x - jnp.max(x, axis=-1, keepdims=True))
    predicted = e * (1.0 / jnp.sum(e, axis=-1, keepdims=True))
    frame = first + lax.broadcasted_iota(jnp.int32, (R, 1), 0)
    valid = jnp.where(frame < s_len, 16.0, 0.0)
    to_body.wait_recv()
    to_tail.wait_recv()
    targets = mm(pick, ext[...])
    total = jnp.sum(targets, axis=-1, keepdims=True)
    lgrad[...] = (valid * (total * predicted - targets)).astype(BF16)

    qc.a(0)

    def s_hidden_grad(i):
        at = cols(i, 256)
        hid[:, at] = mm(lgrad[...], ws[at, pl.ds(DS, VOCAB)], NT).astype(BF16)

    project(0, DS // 256, s_hidden_grad)

    def s_mix_grad(i):
        at = cols(i, 256)
        m = mm(hid[:, pl.ds(0, DS)], ws[at, pl.ds(0, DS)], NT).astype(BF16)
        qm[1, pl.ds(0, R), at] = m
        prod = m.astype(F32) * mix_s[:, at]
        st = stat_c[...]
        for p in range(2):
            part = prod[:, p * 128 : (p + 1) * 128]
            zero = jnp.zeros_like(part)
            in0 = jnp.sum(jnp.where(low, part, zero), axis=-1, keepdims=True)
            in1 = jnp.sum(jnp.where(low, zero, part), axis=-1, keepdims=True)
            st = jnp.where(lane == 16 + 4 * i + 2 * p, in0, st)
            st = jnp.where(lane == 17 + 4 * i + 2 * p, in1, st)
        stat_c[...] = st

        @pl.when(i == 0)
        def _():
            mc.start(0)
            mc.start(1)

        @pl.when(i == 1)
        def _():
            mc.start(2)

    project(0, DS // 256, s_mix_grad)
    stat[:, pl.ds(0, R)] = stat_c[...].T[:32]
    sc.start(0)
    for c in range(3, SCH):
        mc.start(c)

    def query_pair(j):
        at = cols(j, 128)
        kat = cols(TP + j, 128)
        m = qm[1, pl.ds(0, R), at]
        dp = mm(stacked(m), kv[1, :, kat], NT).reshape(2, R, WIN)
        st = stat_c[...]
        zero = jnp.zeros_like(st)
        in0 = jnp.sum(jnp.where(lane == 16 + 2 * j, st, zero), axis=-1, keepdims=True)
        in1 = jnp.sum(jnp.where(lane == 17 + 2 * j, st, zero), axis=-1, keepdims=True)
        inner = jnp.concatenate([in0[None], in1[None]], axis=0)
        ds = (probs[j] * (dp - inner)).astype(BF16).reshape(2 * R, WIN)
        grads[0, :, at] = (merged(mm(ds, kv[0, :, kat])) * 0.125).astype(BF16)

    def key_pair(j):
        at = cols(j, 128)
        kat = cols(TP + j, 128)
        q = qm[0, :, at]
        m = qm[1, :, at]
        x = scores(kv[0, pl.ds(CTX, R), kat], q, bias_k[...])
        lse = jnp.concatenate([stat[pl.ds(2 * j, 1), :][None], stat[pl.ds(2 * j + 1, 1), :][None]], 0)
        inner = jnp.concatenate(
            [stat[pl.ds(16 + 2 * j, 1), :][None], stat[pl.ds(17 + 2 * j, 1), :][None]], 0
        )
        pr = jnp.exp(x - lse)
        grads[2, :, at] = merged(mm(pr.astype(BF16).reshape(2 * R, WIN), m)).astype(BF16)
        dp = mm(stacked(kv[1, pl.ds(CTX, R), kat]), m, NT).reshape(2, R, WIN)
        ds = (pr * (dp - inner)).astype(BF16).reshape(2 * R, WIN)
        grads[1, :, at] = (merged(mm(ds, q)) * 0.125).astype(BF16)

    def result(i, j):
        at = cols(j, 128)
        return pltpu.make_async_copy(grads.at[i, :, at], out.at[i, :, at], osem.at[i, j])

    def query_step(first_pair, count):
        for p in range(count):
            query_pair(first_pair + p)
        for p in range(count):
            result(0, first_pair + p).start()

    def key_step(first_pair, count):
        for p in range(count):
            mc.c(first_pair + p)
        for p in range(count):
            key_pair(first_pair + p)
        for p in range(count):
            result(1, first_pair + p).start()
            result(2, first_pair + p).start()

    def last_chunk(i, carry):
        query_step(i * 2, 2)
        for p in range(2):
            relay_step(i * 2 + p)
        return carry

    def relay_step(i):
        mc.a(i)

        @pl.when(i == 2)
        def _():
            sc.a(0)

        @pl.when(i >= 3)
        def _():
            mc.b(i - 3)

        @pl.when(i == 5)
        def _():
            sc.b(0)

    lax.fori_loop(0, SP // 2, last_chunk, 0)
    mc.b(5)
    qc.b(0)
    sc.c(0)
    qc.c(0)

    def rest(i, carry):
        key_step(i * 2, 2)

        @pl.when(i < 2)
        def _():
            mc.b(i + 6)

        return carry

    lax.fori_loop(0, SP // 2, rest, 0)

    def kv_sent(c, carry):
        kvc.sent(c)
        return carry

    lax.fori_loop(0, NCH, kv_sent, 0)

    def m_sent(c, carry):
        mc.sent(c)
        return carry

    lax.fori_loop(0, SCH, m_sent, 0)
    def results(j, carry):
        for i in range(3):
            result(i, j).wait()
        return carry

    lax.fori_loop(0, SP, results, 0)
    qc.sent(0)
    sc.sent(0)
    to_body.wait_send()
    to_next.wait_send()
    to_tail.wait_send()
    for k in range(6):
        across(k).wait_send()
        for kind in (0, 1, 2) if k < 4 else kinds(k):
            along(k, kind).wait_send()
        for which in pieces(k):
            other_core(k, which).wait_send()


def on_device(*args):
    ns = lax.axis_size("seq")
    args = list(args)
    args[6] = args[6].reshape(1, VOCAB)
    args[13] = args[13].reshape(1, VOCAB)
    hbm = pl.BlockSpec(memory_space=pl.ANY)
    vmem = pl.BlockSpec(memory_space=pltpu.VMEM)
    smem = pl.BlockSpec(memory_space=pltpu.SMEM)
    in_specs = [hbm] * 16
    in_specs[6] = vmem
    in_specs[13] = vmem
    in_specs[14] = smem
    in_specs[15] = vmem
    out = jax.ShapeDtypeStruct((3, R, DS), BF16)
    dma = pltpu.SemaphoreType.DMA
    grads = pl.pallas_call(
        functools.partial(kernel, ns),
        out_shape=out,
        in_specs=in_specs,
        out_specs=hbm,
        scratch_shapes=[
            pltpu.VMEM((3, R, DS), BF16),
            pltpu.VMEM((2, WIN, DT + DS), BF16),
            pltpu.VMEM((R, DT), BF16),
            pltpu.VMEM((R, DT), BF16),
            pltpu.VMEM((R, DS), BF16),
            pltpu.VMEM((DT, DT + VOCAB), BF16),
            pltpu.VMEM((DS, DS + VOCAB), BF16),
            pltpu.VMEM((2, WIN, DS), BF16),
            pltpu.VMEM((SP, 2, R, WIN), F32),
            pltpu.VMEM((R, DT), BF16),
            pltpu.VMEM((R, DS), BF16),
            pltpu.VMEM((R, DS), F32),
            pltpu.VMEM((R, DT), BF16),
            pltpu.VMEM((R, VOCAB), F32),
            pltpu.VMEM((R, VOCAB), BF16),
            pltpu.VMEM((2 * R, VOCAB), BF16),
            pltpu.VMEM((MAXD, VOCAB), BF16),
            pltpu.VMEM((R, VOCAB), BF16),
            pltpu.VMEM((R, WIN), F32),
            pltpu.VMEM((R, WIN), F32),
            pltpu.VMEM((R, WIN), F32),
            pltpu.VMEM((R, 128), F32),
            pltpu.VMEM((32, WIN), F32),
            dma((12,)),
            dma((3, SP)),
            dma((4, NCH)),
            dma((4, NCH)),
            dma((4, 1)),
            dma((4, 1)),
            dma((4, SCH)),
            dma((4, SCH)),
            dma((4, 1)),
            dma((4, 1)),
            dma((6,)),
            dma((6,)),
            dma((3, 6)),
            dma((3, 6)),
            dma((4, 6)),
            dma((4, 6)),
            dma((3,)),
            dma((3,)),
        ],
        compiler_params=pltpu.CompilerParams(
            collective_id=0, has_side_effects=True, vmem_limit_bytes=56 * 1024 * 1024
        ),
    )(*args)
    return grads[0:1], grads[1:2], grads[2:3]


def solution(mesh):
    return jax.shard_map(
        on_device,
        mesh=mesh,
        in_specs=(
            P("grp", "seq", None),
            P("grp", "seq", None),
            P("grp", "seq", None),
            P("grp", "seq", None),
            P("grp", None),
            P("grp", None),
            P(),
            P("grp", "seq", None),
            P("grp", "seq", None),
            P("grp", "seq", None),
            P("grp", "seq", None),
            P("grp", None),
            P("grp", None),
            P(),
            P(),
            P("grp", "seq"),
        ),
        out_specs=(P("grp", "seq", None), P("grp", "seq", None), P("grp", "seq", None)),
        check_vma=False,
    )
```
